32 devices in a mesh: index: 16 (over z, y, x), query: 2 (over core).
Axes of the slice: x: 2, y: 2, z: 4, core: 2. Of those that a mesh axis runs over, the one named last changes fastest.
Arguments:
- queries: bfloat16 [64, 32, 128], P('query'), may hold values from -6 to 6
- passages: bfloat16 [2048, 128, 128], P(('index', 'query')), may hold values from -0.5 to 0.5
- lengths: int32 [2048], P(('index', 'query')), may hold values from 1 to 128
- candidates: int32 [64, 256], P('query', 'index'), may hold values from 0 to 2047, as said below
Outputs:
- scores: float32 [64, 256], P('query', 'index')
The draws below stay inside these ranges and needn't reach their ends.
Inputs may be any that keep to these rules, and one draw needn't show every extreme that they name: Block b is stored on the device of flat position b // 64 along index+query. The 32 x 16 candidates held by one device name blocks of any one storing device at most 32 times, and exactly 32 times for some storing device.
All inputs are finite; a program needn't handle non-finite values.
Results may differ from the reference program's by a relative error of at most 0.0003.
Values may be sent and summed in bfloat16 or wider, within the bound.
A program may use at most 64 MiB of HBM per device.

```python
import jax
import jax.numpy as jnp
from jax import lax

DIM = 128
QT = 32
PTOK = 128
BLK_DEV = 64
Q_DEV = 32
CAND_DEV = 16
CAP = 32
NQ = 64
CAND = 256
BLOCKS = 2048


def draw_candidates(key, part):
    groups_q = NQ // Q_DEV
    groups_i = CAND // CAND_DEV
    owners = BLOCKS // BLK_DEV
    total_slots = owners * CAP
    request_count = Q_DEV * CAND_DEV

    def single(dev_key):
        key_first, key_order, key_mix, key_local = jax.random.split(dev_key, 4)
        first_owner = jax.random.randint(key_first, (), 0, owners)
        ranking = jax.random.permutation(key_order, total_slots).astype(jnp.int32)
        slot_owner = jnp.arange(total_slots, dtype=jnp.int32) // CAP
        ranking = ranking + total_slots * (slot_owner != first_owner).astype(jnp.int32)
        picked = jnp.argsort(ranking)[:request_count].astype(jnp.int32)
        picked = jax.random.permutation(key_mix, picked)
        local_block = jax.random.randint(key_local, (request_count,), 0, BLK_DEV)
        return picked // CAP * BLK_DEV + local_block
    dev_keys = jax.random.split(key, groups_q * groups_i)
    blocks_all = jax.vmap(single)(dev_keys).reshape(groups_q, groups_i, Q_DEV, CAND_DEV)
    return blocks_all.transpose(0, 2, 1, 3).reshape(NQ, CAND).astype(jnp.int32)


def with_ends(entries, own_key, smallest, top_value):
    index_at = [jax.random.randint(jax.random.fold_in(own_key, axis), (), 0, length) for axis, length in enumerate(entries.shape)]
    main_axis = entries.shape.index(max(entries.shape))
    next_to = index_at[:main_axis] + [(index_at[main_axis] + 1) % entries.shape[main_axis]] + index_at[main_axis + 1:]
    return entries.at[tuple(index_at)].set(smallest).at[tuple(next_to)].set(top_value)


def shard_levels(key, dims, pieces, smallest, top_value):
    level = 1.0
    for axis_at, parts in pieces:
        draws = jax.random.uniform(jax.random.fold_in(jax.random.fold_in(key, 6), axis_at), (parts,), jnp.float32, smallest / len(pieces), top_value / len(pieces))
        level = level * jnp.repeat(jnp.exp(draws), dims[axis_at] // parts).reshape((-1,) + (1,) * (len(dims) - 1 - axis_at))
    return level


def gaussian(key, extent, deviation, bound, cuts=(), held_as=jnp.bfloat16):
    level = shard_levels(key, extent, cuts, -0.22, 0.18) if cuts else 1.0
    drawn = jax.random.normal(key, extent, jnp.float32) * deviation * level
    return jnp.minimum(jnp.maximum(drawn, -bound), bound).astype(held_as)


def setup_inputs(seed: int = 0) -> dict:
    streams_of = jax.random.split(jax.random.key(seed), 5)
    queries = gaussian(streams_of[0], (NQ, QT, DIM), 1.0, 6.0, ((0, 2),))
    passages = gaussian(streams_of[1], (BLOCKS, PTOK, DIM), DIM ** -0.5, 0.5, ((0, 32),))
    lengths = with_ends(jax.random.randint(streams_of[2], (BLOCKS,), 1, PTOK + 1), jax.random.fold_in(streams_of[2], 1), 1, PTOK).astype(jnp.int32)
    candidates = draw_candidates(jax.random.fold_in(streams_of[4], 71), 0)
    return {"queries": queries, "passages": passages, "lengths": lengths, "candidates": candidates}


def reference(queries, passages, lengths, candidates):
    token_pos = jnp.arange(passages.shape[1]).astype(jnp.int32)

    def per_query(packed):
        query_rows, chosen = packed
        block_rows = passages[chosen].astype(jnp.float32)
        similar = jnp.einsum("td,cpd->ctp", query_rows.astype(jnp.float32), block_rows)
        live = token_pos[None, None, :] < lengths[chosen][:, None, None]
        best = jnp.max(jnp.where(live, similar, -jnp.inf), axis=2)
        return jnp.mean(best, axis=1)

    return lax.map(per_query, (queries, candidates))
```

```python
import functools

import jax
import jax.numpy as jnp
from jax import lax
from jax.experimental import pallas as pl
from jax.experimental.pallas import tpu as pltpu
from jax.sharding import PartitionSpec as P

MESH = pl.DeviceIdType.MESH
LANES = 128
SUB = 8


def maxsim_kernel(
    n_index,
    n_query,
    q_hbm,
    p_hbm,
    len_ref,
    cand_ref,
    out_ref,
    q_buf,
    p_buf,
    qt_buf,
    best,
    sent,
    table,
    wide,
    q_sem,
    p_sem,
    q_send,
    q_recv,
    s_send,
    s_recv,
):
    me_i = lax.axis_index("index")
    me_q = lax.axis_index("query")
    n_dev = n_index * n_query
    my_slot = me_i * n_query + me_q
    groups, rows, dim = p_buf.shape
    blk_local = len_ref.shape[0]
    per_group = blk_local // groups
    tokens = rows // per_group
    q_rows = q_buf.shape[1]
    halves = sent.shape[1]
    part = q_rows // halves
    half = part // 2
    q_tok = half // SUB
    cand_local = cand_ref.shape[1]

    q_in = pltpu.make_async_copy(q_hbm, q_buf.at[0], q_sem)
    q_in.start()

    def p_copy(g):
        return pltpu.make_async_copy(p_hbm.at[g], p_buf.at[g], p_sem.at[g])

    for g in range(groups):
        p_copy(g).start()

    barrier = pltpu.get_barrier_semaphore()

    def greet(j, carry):
        other = lax.rem(my_slot + j, n_dev)
        pl.semaphore_signal(
            barrier,
            inc=1,
            device_id=(other // n_query, lax.rem(other, n_query)),
            device_id_type=MESH,
        )
        return carry

    lax.fori_loop(1, n_dev, greet, 0)

    token_pos = lax.broadcasted_iota(jnp.int32, (tokens, dim), 0)
    lane_q = lax.broadcasted_iota(jnp.int32, (SUB, half), 1) // q_tok
    row_q = lax.broadcasted_iota(jnp.int32, (SUB, half), 0)
    mean_w = jnp.where(lane_q == row_q, 1.0 / q_tok, 0.0).astype(jnp.bfloat16)

    def score_pass(k, m, first):
        qt_buf[...] = q_buf[k, pl.ds(m * part, part), :].T

        def group_step(g, carry):
            if first:
                p_copy(g).wait()
                for b in range(per_group):
                    block = p_buf[g, pl.ds(b * tokens, tokens), :].astype(jnp.float32)
                    live = token_pos < len_ref[g * per_group + b]
                    block = jnp.where(live, block, block[0:1, :])
                    p_buf[g, pl.ds(b * tokens, tokens), :] = block.astype(jnp.bfloat16)
            similar = jnp.dot(p_buf[g], qt_buf[...], preferred_element_type=jnp.float32)
            top = jnp.max(similar.reshape(per_group, tokens, part), axis=1)
            best[pl.ds(pl.multiple_of(g * per_group, per_group), per_group), :] = top[:, :half]
            best[
                pl.ds(pl.multiple_of(blk_local + g * per_group, per_group), per_group), :
            ] = top[:, half:]
            return carry

        lax.fori_loop(0, groups, group_step, 0)
        all_best = best[...]
        high = all_best.astype(jnp.bfloat16)
        low = (all_best - high.astype(jnp.float32)).astype(jnp.bfloat16)
        dims = (((1,), (1,)), ((), ()))
        sent[k, m] = lax.dot_general(
            mean_w, high, dims, preferred_element_type=jnp.float32
        ) + lax.dot_general(mean_w, low, dims, preferred_element_type=jnp.float32)

    def send_scores(k, m, own):
        to_q = lax.rem(me_q + k, n_query)

        def send(j, carry):
            pltpu.make_async_remote_copy(
                src_ref=sent.at[k, m],
                dst_ref=table.at[my_slot, m],
                send_sem=s_send,
                recv_sem=s_recv,
                device_id=(lax.rem(me_i + j, n_index), to_q),
                device_id_type=MESH,
            ).start()
            return carry

        lax.fori_loop(1 if own else 0, n_index, send, 0)
        if own:
            pltpu.make_async_copy(sent.at[k, m], table.at[my_slot, m], s_recv).start()

    def q_copy(k):
        return pltpu.make_async_remote_copy(
            src_ref=q_buf.at[0],
            dst_ref=q_buf.at[k],
            send_sem=q_send.at[k],
            recv_sem=q_recv.at[k],
            device_id=(me_i, lax.rem(me_q + n_query - k, n_query)),
            device_id_type=MESH,
        )

    q_in.wait()
    score_pass(0, 0, True)
    pl.semaphore_wait(barrier, n_dev - 1)
    for k in range(1, n_query):
        q_copy(k).start()
    send_scores(0, 0, True)
    for m in range(1, halves):
        score_pass(0, m, False)
        send_scores(0, m, True)

    def other_queries(k, carry):
        q_copy(k).wait_recv()
        for m in range(halves):
            score_pass(k, m, False)
            send_scores(k, m, False)
        return carry

    lax.fori_loop(1, n_query, other_queries, 0)

    wide[...] = jnp.zeros_like(wide)
    wide[:, :cand_local] = cand_ref[...]
    pltpu.make_async_copy(table, table, s_recv).wait()

    q_groups = cand_ref.shape[0] // SUB
    ids = [wide[pl.ds(g * SUB, SUB), :] for g in range(q_groups)]
    owners = [v // blk_local for v in ids]
    lanes = [
        v - o * blk_local + (g % 2) * blk_local for g, (v, o) in enumerate(zip(ids, owners))
    ]

    def pick(o, found):
        here = [table[o, m] for m in range(halves)]
        return tuple(
            jnp.where(
                owners[g] == o,
                jnp.take_along_axis(here[g // 2], lanes[g], axis=1),
                found[g],
            )
            for g in range(q_groups)
        )

    found = lax.fori_loop(
        0, n_dev, pick, tuple(jnp.zeros((SUB, LANES), jnp.float32) for _ in ids), unroll=8
    )
    for g in range(q_groups):
        out_ref[pl.ds(g * SUB, SUB), :] = found[g][:, :cand_local]

    pltpu.make_async_copy(
        table.at[pl.ds(0, n_dev - 1)], table.at[pl.ds(0, n_dev - 1)], s_send
    ).wait()
    for k in range(1, n_query):
        q_copy(k).wait_send()


def shards(n_index, n_query, queries, passages, lengths, candidates):
    q_local, q_tok, dim = queries.shape
    blk_local, tokens, _ = passages.shape
    per_group = SUB
    groups = blk_local // per_group
    q_rows = q_local * q_tok
    part = 2 * SUB * q_tok
    halves = q_rows // part
    n_dev = n_index * n_query
    flops = 2 * n_query * q_rows * blk_local * tokens * dim
    any_spec = pl.BlockSpec(memory_space=pl.ANY)
    vmem = pl.BlockSpec(memory_space=pltpu.VMEM)
    return pl.pallas_call(
        functools.partial(maxsim_kernel, n_index, n_query),
        out_shape=jax.ShapeDtypeStruct(candidates.shape, jnp.float32),
        in_specs=[any_spec, any_spec, pl.BlockSpec(memory_space=pltpu.SMEM), vmem],
        out_specs=vmem,
        scratch_shapes=[
            pltpu.VMEM((n_query, q_rows, dim), jnp.bfloat16),
            pltpu.VMEM((groups, per_group * tokens, dim), jnp.bfloat16),
            pltpu.VMEM((dim, part), jnp.bfloat16),
            pltpu.VMEM((2 * blk_local, part // 2), jnp.float32),
            pltpu.VMEM((n_query, halves, SUB, LANES), jnp.float32),
            pltpu.VMEM((n_dev, halves, SUB, LANES), jnp.float32),
            pltpu.VMEM((q_local, LANES), jnp.int32),
            pltpu.SemaphoreType.DMA,
            pltpu.SemaphoreType.DMA((groups,)),
            pltpu.SemaphoreType.DMA((n_query,)),
            pltpu.SemaphoreType.DMA((n_query,)),
            pltpu.SemaphoreType.DMA,
            pltpu.SemaphoreType.DMA,
        ],
        compiler_params=pltpu.CompilerParams(
            collective_id=0, has_side_effects=True, vmem_limit_bytes=40 * 1024 * 1024
        ),
        cost_estimate=pl.CostEstimate(
            flops=flops, bytes_accessed=passages.size * 2, transcendentals=0
        ),
        name="maxsim",
    )(
        queries.reshape(q_rows, dim),
        passages.reshape(groups, per_group * tokens, dim),
        lengths,
        candidates,
    )


def solution(mesh):
    in_specs = (
        P("query", None, None),
        P(("index", "query"), None, None),
        P(("index", "query")),
        P("query", "index"),
    )
    body = functools.partial(shards, mesh.shape["index"], mesh.shape["query"])
    return jax.shard_map(
        body, mesh=mesh, in_specs=in_specs, out_specs=P("query", "index"), check_vma=False
    )
```

```python
import functools

import jax
import jax.numpy as jnp
from jax import lax
from jax.experimental import pallas as pl
from jax.experimental.pallas import tpu as pltpu
from jax.sharding import PartitionSpec as P

MESH = pl.DeviceIdType.MESH
LANES = 128
SUB = 8


def maxsim_kernel(
    n_index,
    n_query,
    q_hbm,
    p_hbm,
    len_hbm,
    cand_hbm,
    out_ref,
    len_ref,
    cand_ref,
    q_buf,
    p_buf,
    qt_buf,
    best,
    sent,
    table,
    wide,
    q_sem,
    p_sem,
    q_send,
    q_recv,
    s_send,
    s_recv,
    len_sem,
    cand_sem,
):
    me_i = lax.axis_index("index")
    me_q = lax.axis_index("query")
    n_dev = n_index * n_query
    my_slot = me_i * n_query + me_q
    groups, rows, dim = p_buf.shape
    blk_local = len_ref.shape[0]
    per_group = blk_local // groups
    tokens = rows // per_group
    q_rows = q_buf.shape[1]
    halves = sent.shape[1]
    part = q_rows // halves
    half = part // 2
    q_tok = half // SUB
    cand_local = cand_ref.shape[0]

    q_in = pltpu.make_async_copy(q_hbm, q_buf.at[0], q_sem)
    q_in.start()
    len_in = pltpu.make_async_copy(len_hbm, len_ref, len_sem)
    len_in.start()

    def p_copy(g):
        return pltpu.make_async_copy(p_hbm.at[g], p_buf.at[g], p_sem.at[g])

    for g in range(groups):
        p_copy(g).start()
    cand_in = pltpu.make_async_copy(cand_hbm, cand_ref, cand_sem)
    cand_in.start()

    barrier = pltpu.get_barrier_semaphore()

    def greet(j, carry):
        other = lax.rem(my_slot + j, n_dev)
        pl.semaphore_signal(
            barrier,
            inc=1,
            device_id=(other // n_query, lax.rem(other, n_query)),
            device_id_type=MESH,
        )
        return carry

    lax.fori_loop(1, n_dev, greet, 0)

    token_pos = lax.broadcasted_iota(jnp.int32, (tokens, dim), 0)
    lane_q = lax.broadcasted_iota(jnp.int32, (SUB, half), 1) // q_tok
    row_q = lax.broadcasted_iota(jnp.int32, (SUB, half), 0)
    mean_w = jnp.where(lane_q == row_q, 1.0 / q_tok, 0.0).astype(jnp.bfloat16)

    def score_pass(k, m, first):
        qt_buf[...] = q_buf[k, pl.ds(m * part, part), :].T

        def group_step(g, carry):
            if first:
                p_copy(g).wait()
                blocks = []
                for b in range(per_group):
                    block = p_buf[g, pl.ds(b * tokens, tokens), :].astype(jnp.float32)
                    live = token_pos < len_ref[g * per_group + b]
                    blocks.append(jnp.where(live, block, block[0:1, :]).astype(jnp.bfloat16))
                group_rows = jnp.concatenate(blocks, axis=0)
                p_buf[g] = group_rows
            else:
                group_rows = p_buf[g]
            similar = jnp.dot(group_rows, qt_buf[...], preferred_element_type=jnp.float32)
            top = jnp.max(similar.reshape(per_group, tokens, part), axis=1)
            best[pl.ds(pl.multiple_of(g * per_group, per_group), per_group), :] = top[:, :half]
            best[
                pl.ds(pl.multiple_of(blk_local + g * per_group, per_group), per_group), :
            ] = top[:, half:]
            return carry

        lax.fori_loop(0, groups, group_step, 0, unroll=2)
        all_best = best[...]
        high = all_best.astype(jnp.bfloat16)
        low = (all_best - high.astype(jnp.float32)).astype(jnp.bfloat16)
        dims = (((1,), (1,)), ((), ()))
        sent[k, m] = lax.dot_general(
            mean_w, high, dims, preferred_element_type=jnp.float32
        ) + lax.dot_general(mean_w, low, dims, preferred_element_type=jnp.float32)

    def send_scores(k, m, own):
        to_q = lax.rem(me_q + k, n_query)

        def send(j, carry):
            pltpu.make_async_remote_copy(
                src_ref=sent.at[k, m],
                dst_ref=table.at[my_slot, m],
                send_sem=s_send,
                recv_sem=s_recv,
                device_id=(lax.rem(me_i + j, n_index), to_q),
                device_id_type=MESH,
            ).start()
            return carry

        lax.fori_loop(1 if own else 0, n_index, send, 0)
        if own:
            pltpu.make_async_copy(sent.at[k, m], table.at[my_slot, m], s_recv).start()

    def q_copy(k):
        return pltpu.make_async_remote_copy(
            src_ref=q_buf.at[0],
            dst_ref=q_buf.at[k],
            send_sem=q_send.at[k],
            recv_sem=q_recv.at[k],
            device_id=(me_i, lax.rem(me_q + n_query - k, n_query)),
            device_id_type=MESH,
        )

    q_in.wait()
    len_in.wait()
    score_pass(0, 0, True)
    pl.semaphore_wait(barrier, n_dev - 1)
    for k in range(1, n_query):
        q_copy(k).start()
    send_scores(0, 0, True)
    for m in range(1, halves):
        score_pass(0, m, False)
        send_scores(0, m, True)

    def other_queries(k, carry):
        q_copy(k).wait_recv()
        for m in range(halves):
            score_pass(k, m, False)
            send_scores(k, m, False)
        return carry

    lax.fori_loop(1, n_query, other_queries, 0)

    cand_in.wait()
    wide[...] = jnp.zeros_like(wide)
    wide[:, :cand_local] = cand_ref[...].T
    pltpu.make_async_copy(table, table, s_recv).wait()

    q_groups = cand_ref.shape[1] // SUB
    ids = [wide[pl.ds(g * SUB, SUB), :] for g in range(q_groups)]
    owners = [v // blk_local for v in ids]
    lanes = [
        v - o * blk_local + (g % 2) * blk_local for g, (v, o) in enumerate(zip(ids, owners))
    ]

    def pick(o, found):
        here = [table[o, m] for m in range(halves)]
        return tuple(
            jnp.where(
                owners[g] == o,
                jnp.take_along_axis(here[g // 2], lanes[g], axis=1),
                found[g],
            )
            for g in range(q_groups)
        )

    found = lax.fori_loop(
        0, n_dev, pick, tuple(jnp.zeros((SUB, LANES), jnp.float32) for _ in ids), unroll=8
    )
    scores = jnp.concatenate([v[:, :cand_local] for v in found], axis=0)
    out_ref[...] = scores.T

    pltpu.make_async_copy(
        table.at[pl.ds(0, n_dev - 1)], table.at[pl.ds(0, n_dev - 1)], s_send
    ).wait()
    for k in range(1, n_query):
        q_copy(k).wait_send()


def shards(n_index, n_query, queries, passages, lengths, candidates):
    q_local, q_tok, dim = queries.shape
    blk_local, tokens, _ = passages.shape
    per_group = SUB
    groups = blk_local // per_group
    q_rows = q_local * q_tok
    part = 2 * SUB * q_tok
    halves = q_rows // part
    n_dev = n_index * n_query
    flops = 2 * n_query * q_rows * blk_local * tokens * dim
    hbm = pl.BlockSpec(memory_space=pltpu.HBM)
    vmem = pl.BlockSpec(memory_space=pltpu.VMEM)
    return pl.pallas_call(
        functools.partial(maxsim_kernel, n_index, n_query),
        out_shape=jax.ShapeDtypeStruct(candidates.shape[::-1], jnp.float32),
        in_specs=[hbm, hbm, hbm, hbm],
        out_specs=vmem,
        scratch_shapes=[
            pltpu.SMEM(lengths.shape, jnp.int32),
            pltpu.VMEM(candidates.shape[::-1], jnp.int32),
            pltpu.VMEM((n_query, q_rows, dim), jnp.bfloat16),
            pltpu.VMEM((groups, per_group * tokens, dim), jnp.bfloat16),
            pltpu.VMEM((dim, part), jnp.bfloat16),
            pltpu.VMEM((2 * blk_local, part // 2), jnp.float32),
            pltpu.VMEM((n_query, halves, SUB, LANES), jnp.float32),
            pltpu.VMEM((n_dev, halves, SUB, LANES), jnp.float32),
            pltpu.VMEM((q_local, LANES), jnp.int32),
            pltpu.SemaphoreType.DMA,
            pltpu.SemaphoreType.DMA((groups,)),
            pltpu.SemaphoreType.DMA((n_query,)),
            pltpu.SemaphoreType.DMA((n_query,)),
            pltpu.SemaphoreType.DMA,
            pltpu.SemaphoreType.DMA,
            pltpu.SemaphoreType.DMA,
            pltpu.SemaphoreType.DMA,
        ],
        compiler_params=pltpu.CompilerParams(
            collective_id=0, has_side_effects=True, vmem_limit_bytes=60 * 1024 * 1024
        ),
        cost_estimate=pl.CostEstimate(
            flops=flops, bytes_accessed=passages.size * 2, transcendentals=0
        ),
        name="maxsim",
    )(
        queries.reshape(q_rows, dim),
        passages.reshape(groups, per_group * tokens, dim),
        lengths,
        candidates.T,
    ).T


def solution(mesh):
    in_specs = (
        P("query", None, None),
        P(("index", "query"), None, None),
        P(("index", "query")),
        P("query", "index"),
    )
    body = functools.partial(shards, mesh.shape["index"], mesh.shape["query"])
    return jax.shard_map(
        body, mesh=mesh, in_specs=in_specs, out_specs=P("query", "index"), check_vma=False
    )
```

```python
import functools

import jax
import jax.numpy as jnp
from jax import lax
from jax.experimental import pallas as pl
from jax.experimental.pallas import tpu as pltpu
from jax.sharding import PartitionSpec as P

MESH = pl.DeviceIdType.MESH
LANES = 128
SUB = 8


def maxsim_kernel(
    n_index,
    n_query,
    q_hbm,
    p_hbm,
    len_hbm,
    cand_hbm,
    out_ref,
    len_ref,
    cand_ref,
    q_buf,
    p_buf,
    qt_buf,
    best,
    sent,
    table,
    wide,
    q_sem,
    p_sem,
    q_send,
    q_recv,
    s_send,
    s_recv,
    len_sem,
    cand_sem,
):
    me_i = lax.axis_index("index")
    me_q = lax.axis_index("query")
    n_dev = n_index * n_query
    my_slot = me_i * n_query + me_q
    groups, rows, dim = p_buf.shape
    blk_local = len_ref.shape[0]
    per_group = blk_local // groups
    tokens = rows // per_group
    q_rows = q_buf.shape[1]
    halves = sent.shape[1]
    part = q_rows // halves
    half = part // 2
    q_tok = half // SUB
    cand_local = cand_ref.shape[0]

    q_in = pltpu.make_async_copy(q_hbm, q_buf.at[0], q_sem)
    q_in.start()
    len_in = pltpu.make_async_copy(len_hbm, len_ref, len_sem)
    len_in.start()

    def p_copy(g):
        return pltpu.make_async_copy(p_hbm.at[g], p_buf.at[g], p_sem.at[g])

    for g in range(groups):
        p_copy(g).start()
    cand_in = pltpu.make_async_copy(cand_hbm, cand_ref, cand_sem)
    cand_in.start()

    barrier = pltpu.get_barrier_semaphore()

    def greet(j, carry):
        other = lax.rem(my_slot + j, n_dev)
        pl.semaphore_signal(
            barrier,
            inc=1,
            device_id=(other // n_query, lax.rem(other, n_query)),
            device_id_type=MESH,
        )
        return carry

    lax.fori_loop(1, n_dev, greet, 0)

    token_pos = lax.broadcasted_iota(jnp.int32, (tokens, dim), 0)
    lane_q = lax.broadcasted_iota(jnp.int32, (SUB, half), 1) // q_tok
    row_q = lax.broadcasted_iota(jnp.int32, (SUB, half), 0)
    mean_w = jnp.where(lane_q == row_q, 1.0 / q_tok, 0.0).astype(jnp.bfloat16)

    def score_pass(k, m, first):
        qt_buf[...] = q_buf[k, pl.ds(pl.multiple_of(m * part, part), part), :].T

        def group_step(g, carry):
            if first:
                p_copy(g).wait()
                blocks = []
                for b in range(per_group):
                    block = p_buf[g, pl.ds(b * tokens, tokens), :].astype(jnp.float32)
                    live = token_pos < len_ref[g * per_group + b]
                    blocks.append(jnp.where(live, block, block[0:1, :]).astype(jnp.bfloat16))
                group_rows = jnp.concatenate(blocks, axis=0)
                p_buf[g] = group_rows
            else:
                group_rows = p_buf[g]
            similar = jnp.dot(group_rows, qt_buf[...], preferred_element_type=jnp.float32)
            top = jnp.max(similar.reshape(per_group, tokens, part), axis=1)
            best[pl.ds(pl.multiple_of(g * per_group, per_group), per_group), :] = top[:, :half]
            best[
                pl.ds(pl.multiple_of(blk_local + g * per_group, per_group), per_group), :
            ] = top[:, half:]
            return carry

        lax.fori_loop(0, groups, group_step, 0, unroll=4)
        all_best = best[...]
        high = all_best.astype(jnp.bfloat16)
        low = (all_best - high.astype(jnp.float32)).astype(jnp.bfloat16)
        dims = (((1,), (1,)), ((), ()))
        sent[k, m] = lax.dot_general(
            mean_w, high, dims, preferred_element_type=jnp.float32
        ) + lax.dot_general(mean_w, low, dims, preferred_element_type=jnp.float32)

    def send_scores(k, m):
        to_q = lax.rem(me_q + k, n_query)
        own = jnp.where(k == 0, 1, 0)

        def send(j, carry):
            pltpu.make_async_remote_copy(
                src_ref=sent.at[k, m],
                dst_ref=table.at[my_slot, m],
                send_sem=s_send,
                recv_sem=s_recv,
                device_id=(lax.rem(me_i + j, n_index), to_q),
                device_id_type=MESH,
            ).start()
            return carry

        lax.fori_loop(own, n_index, send, 0)

        @pl.when(own == 1)
        def _():
            pltpu.make_async_copy(sent.at[k, m], table.at[my_slot, m], s_recv).start()

    def q_copy(k):
        return pltpu.make_async_remote_copy(
            src_ref=q_buf.at[0],
            dst_ref=q_buf.at[k],
            send_sem=q_send.at[k],
            recv_sem=q_recv.at[k],
            device_id=(me_i, lax.rem(me_q + n_query - k, n_query)),
            device_id_type=MESH,
        )

    q_in.wait()
    len_in.wait()
    score_pass(0, 0, True)
    pl.semaphore_wait(barrier, n_dev - 1)
    for k in range(1, n_query):
        q_copy(k).start()
    send_scores(0, 0)

    def later_pass(step, carry):
        k = step // halves
        m = lax.rem(step, halves)

        @pl.when((k > 0) & (m == 0))
        def _():
            q_copy(k).wait_recv()

        score_pass(k, m, False)
        send_scores(k, m)
        return carry

    lax.fori_loop(1, n_query * halves, later_pass, 0)

    cand_in.wait()
    wide[...] = jnp.zeros_like(wide)
    wide[:, :cand_local] = cand_ref[...].T
    pltpu.make_async_copy(table, table, s_recv).wait()

    q_groups = cand_ref.shape[1] // SUB
    ids = [wide[pl.ds(g * SUB, SUB), :] for g in range(q_groups)]
    owners = [v // blk_local for v in ids]
    lanes = [
        v - o * blk_local + (g % 2) * blk_local for g, (v, o) in enumerate(zip(ids, owners))
    ]

    def pick(o, found):
        here = [table[o, m] for m in range(halves)]
        return tuple(
            jnp.where(
                owners[g] == o,
                jnp.take_along_axis(here[g // 2], lanes[g], axis=1),
                found[g],
            )
            for g in range(q_groups)
        )

    found = lax.fori_loop(
        0, n_dev, pick, tuple(jnp.zeros((SUB, LANES), jnp.float32) for _ in ids), unroll=8
    )
    scores = jnp.concatenate([v[:, :cand_local] for v in found], axis=0)
    out_ref[...] = scores.T

    pltpu.make_async_copy(
        table.at[pl.ds(0, n_dev - 1)], table.at[pl.ds(0, n_dev - 1)], s_send
    ).wait()
    for k in range(1, n_query):
        q_copy(k).wait_send()


def shards(n_index, n_query, queries, passages, lengths, candidates):
    q_local, q_tok, dim = queries.shape
    blk_local, tokens, _ = passages.shape
    per_group = SUB
    groups = blk_local // per_group
    q_rows = q_local * q_tok
    part = 2 * SUB * q_tok
    halves = q_rows // part
    n_dev = n_index * n_query
    flops = 2 * n_query * q_rows * blk_local * tokens * dim
    hbm = pl.BlockSpec(memory_space=pltpu.HBM)
    vmem = pl.BlockSpec(memory_space=pltpu.VMEM)
    return pl.pallas_call(
        functools.partial(maxsim_kernel, n_index, n_query),
        out_shape=jax.ShapeDtypeStruct(candidates.shape[::-1], jnp.float32),
        in_specs=[hbm, hbm, hbm, hbm],
        out_specs=vmem,
        scratch_shapes=[
            pltpu.SMEM(lengths.shape, jnp.int32),
            pltpu.VMEM(candidates.shape[::-1], jnp.int32),
            pltpu.VMEM((n_query, q_rows, dim), jnp.bfloat16),
            pltpu.VMEM((groups, per_group * tokens, dim), jnp.bfloat16),
            pltpu.VMEM((dim, part), jnp.bfloat16),
            pltpu.VMEM((2 * blk_local, part // 2), jnp.float32),
            pltpu.VMEM((n_query, halves, SUB, LANES), jnp.float32),
            pltpu.VMEM((n_dev, halves, SUB, LANES), jnp.float32),
            pltpu.VMEM((q_local, LANES), jnp.int32),
            pltpu.SemaphoreType.DMA,
            pltpu.SemaphoreType.DMA((groups,)),
            pltpu.SemaphoreType.DMA((n_query,)),
            pltpu.SemaphoreType.DMA((n_query,)),
            pltpu.SemaphoreType.DMA,
            pltpu.SemaphoreType.DMA,
            pltpu.SemaphoreType.DMA,
            pltpu.SemaphoreType.DMA,
        ],
        compiler_params=pltpu.CompilerParams(
            collective_id=0, has_side_effects=True, vmem_limit_bytes=60 * 1024 * 1024
        ),
        cost_estimate=pl.CostEstimate(
            flops=flops, bytes_accessed=passages.size * 2, transcendentals=0
        ),
        name="maxsim",
    )(
        queries.reshape(q_rows, dim),
        passages.reshape(groups, per_group * tokens, dim),
        lengths,
        candidates.T,
    ).T


def solution(mesh):
    in_specs = (
        P("query", None, None),
        P(("index", "query"), None, None),
        P(("index", "query")),
        P("query", "index"),
    )
    body = functools.partial(shards, mesh.shape["index"], mesh.shape["query"])
    return jax.shard_map(
        body, mesh=mesh, in_specs=in_specs, out_specs=P("query", "index"), check_vma=False
    )
```

```python
import functools

import jax
import jax.numpy as jnp
from jax import lax
from jax.experimental import pallas as pl
from jax.experimental.pallas import tpu as pltpu
from jax.sharding import PartitionSpec as P

MESH = pl.DeviceIdType.MESH
LANES = 128
SUB = 8


def maxsim_kernel(
    n_index,
    n_query,
    q_hbm,
    p_hbm,
    len_hbm,
    cand_hbm,
    out_ref,
    len_ref,
    cand_ref,
    q_buf,
    p_buf,
    qt_buf,
    best,
    sent,
    table,
    wide,
    q_sem,
    p_sem,
    q_send,
    q_recv,
    s_send,
    s_recv,
    len_sem,
    cand_sem,
):
    me_i = lax.axis_index("index")
    me_q = lax.axis_index("query")
    n_dev = n_index * n_query
    my_slot = me_i * n_query + me_q
    groups, rows, dim = p_buf.shape
    blk_local = len_ref.shape[0]
    per_group = blk_local // groups
    tokens = rows // per_group
    q_rows = q_buf.shape[1]
    halves = sent.shape[1]
    part = q_rows // halves
    half = part // 2
    q_tok = half // SUB
    cand_local = cand_ref.shape[0]

    q_in = pltpu.make_async_copy(q_hbm, q_buf.at[0], q_sem)
    q_in.start()
    len_in = pltpu.make_async_copy(len_hbm, len_ref, len_sem)
    len_in.start()

    def p_copy(g):
        return pltpu.make_async_copy(p_hbm.at[g], p_buf.at[g], p_sem.at[g])

    for g in range(groups):
        p_copy(g).start()
    cand_in = pltpu.make_async_copy(cand_hbm, cand_ref, cand_sem)
    cand_in.start()

    barrier = pltpu.get_barrier_semaphore()

    def greet(j, carry):
        other = lax.rem(my_slot + j, n_dev)
        pl.semaphore_signal(
            barrier,
            inc=1,
            device_id=(other // n_query, lax.rem(other, n_query)),
            device_id_type=MESH,
        )
        return carry

    lax.fori_loop(1, n_dev, greet, 0)

    token_pos = lax.broadcasted_iota(jnp.int32, (tokens, dim), 0)
    lane_q = lax.broadcasted_iota(jnp.int32, (SUB, half), 1) // q_tok
    row_q = lax.broadcasted_iota(jnp.int32, (SUB, half), 0)
    mean_w = jnp.where(lane_q == row_q, 1.0 / q_tok, 0.0).astype(jnp.bfloat16)

    def score_pass(k, m, first):
        qt_buf[...] = q_buf[k, pl.ds(pl.multiple_of(m * part, part), part), :].T

        def group_step(g, carry):
            if first:
                p_copy(g).wait()
                blocks = []
                for b in range(per_group):
                    block = p_buf[g, pl.ds(b * tokens, tokens), :].astype(jnp.float32)
                    live = token_pos < len_ref[g * per_group + b]
                    blocks.append(jnp.where(live, block, block[0:1, :]).astype(jnp.bfloat16))
                group_rows = jnp.concatenate(blocks, axis=0)
                p_buf[g] = group_rows
            else:
                group_rows = p_buf[g]
            similar = jnp.dot(group_rows, qt_buf[...], preferred_element_type=jnp.float32)
            top = jnp.max(similar.reshape(per_group, tokens, part), axis=1)
            best[pl.ds(pl.multiple_of(g * per_group, per_group), per_group), :] = top[:, :half]
            best[
                pl.ds(pl.multiple_of(blk_local + g * per_group, per_group), per_group), :
            ] = top[:, half:]
            return carry

        lax.fori_loop(0, groups, group_step, 0, unroll=4 if first else 8)
        all_best = best[...]
        high = all_best.astype(jnp.bfloat16)
        low = (all_best - high.astype(jnp.float32)).astype(jnp.bfloat16)
        dims = (((1,), (1,)), ((), ()))
        sent[k, m] = lax.dot_general(
            mean_w, high, dims, preferred_element_type=jnp.float32
        ) + lax.dot_general(mean_w, low, dims, preferred_element_type=jnp.float32)

    def send_scores(k, m):
        to_q = lax.rem(me_q + k, n_query)
        own = jnp.where(k == 0, 1, 0)

        def send(j, carry):
            pltpu.make_async_remote_copy(
                src_ref=sent.at[k, m],
                dst_ref=table.at[my_slot, m],
                send_sem=s_send,
                recv_sem=s_recv,
                device_id=(lax.rem(me_i + j, n_index), to_q),
                device_id_type=MESH,
            ).start()
            return carry

        lax.fori_loop(own, n_index, send, 0)

        @pl.when(own == 1)
        def _():
            pltpu.make_async_copy(sent.at[k, m], table.at[my_slot, m], s_recv).start()

    def q_copy(k):
        return pltpu.make_async_remote_copy(
            src_ref=q_buf.at[0],
            dst_ref=q_buf.at[k],
            send_sem=q_send.at[k],
            recv_sem=q_recv.at[k],
            device_id=(me_i, lax.rem(me_q + n_query - k, n_query)),
            device_id_type=MESH,
        )

    q_in.wait()
    len_in.wait()
    score_pass(0, 0, True)
    pl.semaphore_wait(barrier, n_dev - 1)
    for k in range(1, n_query):
        q_copy(k).start()
    send_scores(0, 0)

    def later_pass(step, carry):
        k = step // halves
        m = lax.rem(step, halves)

        @pl.when((k > 0) & (m == 0))
        def _():
            q_copy(k).wait_recv()

        score_pass(k, m, False)
        send_scores(k, m)
        return carry

    lax.fori_loop(1, n_query * halves, later_pass, 0)

    cand_in.wait()
    wide[...] = jnp.zeros_like(wide)
    wide[:, :cand_local] = cand_ref[...].T
    pltpu.make_async_copy(table, table, s_recv).wait()

    q_groups = cand_ref.shape[1] // SUB
    ids = [wide[pl.ds(g * SUB, SUB), :] for g in range(q_groups)]
    owners = [v // blk_local for v in ids]
    lanes = [
        v - o * blk_local + (g % 2) * blk_local for g, (v, o) in enumerate(zip(ids, owners))
    ]

    def pick(o, found):
        here = [table[o, m] for m in range(halves)]
        return tuple(
            jnp.where(
                owners[g] == o,
                jnp.take_along_axis(here[g // 2], lanes[g], axis=1),
                found[g],
            )
            for g in range(q_groups)
        )

    found = lax.fori_loop(
        0, n_dev, pick, tuple(jnp.zeros((SUB, LANES), jnp.float32) for _ in ids), unroll=8
    )
    scores = jnp.concatenate([v[:, :cand_local] for v in found], axis=0)
    out_ref[...] = scores.T

    pltpu.make_async_copy(
        table.at[pl.ds(0, n_dev - 1)], table.at[pl.ds(0, n_dev - 1)], s_send
    ).wait()
    for k in range(1, n_query):
        q_copy(k).wait_send()


def shards(n_index, n_query, queries, passages, lengths, candidates):
    q_local, q_tok, dim = queries.shape
    blk_local, tokens, _ = passages.shape
    per_group = SUB
    groups = blk_local // per_group
    q_rows = q_local * q_tok
    part = 2 * SUB * q_tok
    halves = q_rows // part
    n_dev = n_index * n_query
    flops = 2 * n_query * q_rows * blk_local * tokens * dim
    hbm = pl.BlockSpec(memory_space=pltpu.HBM)
    vmem = pl.BlockSpec(memory_space=pltpu.VMEM)
    return pl.pallas_call(
        functools.partial(maxsim_kernel, n_index, n_query),
        out_shape=pltpu.VMEM(candidates.shape[::-1], jnp.float32),
        in_specs=[hbm, hbm, hbm, hbm],
        out_specs=vmem,
        scratch_shapes=[
            pltpu.SMEM(lengths.shape, jnp.int32),
            pltpu.VMEM(candidates.shape[::-1], jnp.int32),
            pltpu.VMEM((n_query, q_rows, dim), jnp.bfloat16),
            pltpu.VMEM((groups, per_group * tokens, dim), jnp.bfloat16),
            pltpu.VMEM((dim, part), jnp.bfloat16),
            pltpu.VMEM((2 * blk_local, part // 2), jnp.float32),
            pltpu.VMEM((n_query, halves, SUB, LANES), jnp.float32),
            pltpu.VMEM((n_dev, halves, SUB, LANES), jnp.float32),
            pltpu.VMEM((q_local, LANES), jnp.int32),
            pltpu.SemaphoreType.DMA,
            pltpu.SemaphoreType.DMA((groups,)),
            pltpu.SemaphoreType.DMA((n_query,)),
            pltpu.SemaphoreType.DMA((n_query,)),
            pltpu.SemaphoreType.DMA,
            pltpu.SemaphoreType.DMA,
            pltpu.SemaphoreType.DMA,
            pltpu.SemaphoreType.DMA,
        ],
        compiler_params=pltpu.CompilerParams(
            collective_id=0, has_side_effects=True, vmem_limit_bytes=60 * 1024 * 1024
        ),
        cost_estimate=pl.CostEstimate(
            flops=flops, bytes_accessed=passages.size * 2, transcendentals=0
        ),
        name="maxsim",
    )(
        queries.reshape(q_rows, dim),
        passages.reshape(groups, per_group * tokens, dim),
        lengths,
        candidates.T,
    ).T


def solution(mesh):
    in_specs = (
        P("query", None, None),
        P(("index", "query"), None, None),
        P(("index", "query")),
        P("query", "index"),
    )
    body = functools.partial(shards, mesh.shape["index"], mesh.shape["query"])
    return jax.shard_map(
        body, mesh=mesh, in_specs=in_specs, out_specs=P("query", "index"), check_vma=False
    )
```

```python
import functools

import jax
import jax.numpy as jnp
from jax import lax
from jax.experimental import pallas as pl
from jax.experimental.pallas import tpu as pltpu
from jax.sharding import PartitionSpec as P

MESH = pl.DeviceIdType.MESH
LANES = 128
SUB = 8


def maxsim_kernel(
    n_index,
    n_query,
    q_hbm,
    p_hbm,
    len_hbm,
    cand_hbm,
    out_ref,
    len_ref,
    cand_ref,
    q_buf,
    p_buf,
    qt_buf,
    best,
    sent,
    table,
    wide,
    q_sem,
    p_sem,
    q_send,
    q_recv,
    s_send,
    s_recv,
    len_sem,
    cand_sem,
):
    me_i = lax.axis_index("index")
    me_q = lax.axis_index("query")
    n_dev = n_index * n_query
    my_slot = me_i * n_query + me_q
    groups, rows, dim = p_buf.shape
    blk_local = len_ref.shape[0]
    per_group = blk_local // groups
    tokens = rows // per_group
    q_rows = q_buf.shape[1]
    halves = sent.shape[1]
    part = q_rows // halves
    half = part // 2
    q_tok = half // SUB
    cand_local = cand_ref.shape[0]

    q_in = pltpu.make_async_copy(q_hbm, q_buf.at[0], q_sem)
    q_in.start()
    len_in = pltpu.make_async_copy(len_hbm, len_ref, len_sem)
    len_in.start()

    def p_copy(g):
        return pltpu.make_async_copy(p_hbm.at[g], p_buf.at[g], p_sem.at[g])

    for g in range(groups):
        p_copy(g).start()
    cand_in = pltpu.make_async_copy(cand_hbm, cand_ref, cand_sem)
    cand_in.start()

    barrier = pltpu.get_barrier_semaphore()

    def greet(j, carry):
        other = lax.rem(my_slot + j, n_dev)
        pl.semaphore_signal(
            barrier,
            inc=1,
            device_id=(other // n_query, lax.rem(other, n_query)),
            device_id_type=MESH,
        )
        return carry

    lax.fori_loop(1, n_dev, greet, 0)

    token_pos = lax.broadcasted_iota(jnp.int32, (tokens, dim), 0)
    lane_q = lax.broadcasted_iota(jnp.int32, (SUB, half), 1) // q_tok
    row_q = lax.broadcasted_iota(jnp.int32, (SUB, half), 0)
    mean_w = jnp.where(lane_q == row_q, 1.0 / q_tok, 0.0).astype(jnp.bfloat16)

    def score_pass(k, m, side, first, between):
        qt_buf[...] = q_buf[k, pl.ds(pl.multiple_of(m * part, part), part), :].T
        for g in range(groups):
            if first:
                p_copy(g).wait()
                blocks = []
                for b in range(per_group):
                    block = p_buf[g, pl.ds(b * tokens, tokens), :].astype(jnp.float32)
                    live = token_pos < len_ref[g * per_group + b]
                    blocks.append(jnp.where(live, block, block[0:1, :]).astype(jnp.bfloat16))
                group_rows = jnp.concatenate(blocks, axis=0)
                p_buf[g] = group_rows
            else:
                group_rows = p_buf[g]
            similar = jnp.dot(group_rows, qt_buf[...], preferred_element_type=jnp.float32)
            top = jnp.max(similar.reshape(per_group, tokens, part), axis=1)
            best[side, pl.ds(g * per_group, per_group), :] = top[:, :half]
            best[side, pl.ds(blk_local + g * per_group, per_group), :] = top[:, half:]
            if g == 0:
                between()

    def mean_scores(k, m, side):
        all_best = best[side]
        high = all_best.astype(jnp.bfloat16)
        low = (all_best - high.astype(jnp.float32)).astype(jnp.bfloat16)
        dims = (((1,), (1,)), ((), ()))
        sent[k, m] = lax.dot_general(
            mean_w, high, dims, preferred_element_type=jnp.float32
        ) + lax.dot_general(mean_w, low, dims, preferred_element_type=jnp.float32)

    def send_one(k, m, j):
        pltpu.make_async_remote_copy(
            src_ref=sent.at[k, m],
            dst_ref=table.at[my_slot, m],
            send_sem=s_send,
            recv_sem=s_recv,
            device_id=(lax.rem(me_i + j, n_index), lax.rem(me_q + k, n_query)),
            device_id_type=MESH,
        ).start()

    def send_rest(k, m):
        for j in range(1, n_index):
            send_one(k, m, j)

    def send_near(k, m):
        @pl.when(k > 0)
        def _():
            send_one(k, m, 0)

        @pl.when(k == 0)
        def _():
            pltpu.make_async_copy(sent.at[k, m], table.at[my_slot, m], s_recv).start()

    def q_copy(k):
        return pltpu.make_async_remote_copy(
            src_ref=q_buf.at[0],
            dst_ref=q_buf.at[k],
            send_sem=q_send.at[k],
            recv_sem=q_recv.at[k],
            device_id=(me_i, lax.rem(me_q + n_query - k, n_query)),
            device_id_type=MESH,
        )

    q_in.wait()
    len_in.wait()
    score_pass(0, 0, 0, True, lambda: None)
    pl.semaphore_wait(barrier, n_dev - 1)
    for k in range(1, n_query):
        q_copy(k).start()

    def later_pass(step, carry):
        k = step // halves
        m = lax.rem(step, halves)
        old = step - 1
        old_k = old // halves
        old_m = lax.rem(old, halves)

        @pl.when((k > 0) & (m == 0))
        def _():
            q_copy(k).wait_recv()

        mean_scores(old_k, old_m, lax.rem(old, 2))
        score_pass(k, m, lax.rem(step, 2), False, lambda: send_rest(old_k, old_m))
        send_near(old_k, old_m)
        return carry

    passes = n_query * halves
    lax.fori_loop(1, passes, later_pass, 0)
    last_k, last_m = n_query - 1, halves - 1
    mean_scores(last_k, last_m, (passes - 1) % 2)
    send_rest(last_k, last_m)
    send_near(last_k, last_m)

    cand_in.wait()
    wide[...] = jnp.zeros_like(wide)
    wide[:, :cand_local] = cand_ref[...].T
    q_groups = cand_ref.shape[1] // SUB
    ids = [wide[pl.ds(g * SUB, SUB), :] for g in range(q_groups)]
    owners = [v // blk_local for v in ids]
    lanes = [
        v - o * blk_local + (g % 2) * blk_local for g, (v, o) in enumerate(zip(ids, owners))
    ]

    pltpu.make_async_copy(table, table, s_recv).wait()

    def pick(o, found):
        here = [table[o, m] for m in range(halves)]
        return tuple(
            jnp.where(
                owners[g] == o,
                jnp.take_along_axis(here[g // 2], lanes[g], axis=1),
                found[g],
            )
            for g in range(q_groups)
        )

    found = lax.fori_loop(
        0, n_dev, pick, tuple(jnp.zeros((SUB, LANES), jnp.float32) for _ in ids), unroll=8
    )
    scores = jnp.concatenate([v[:, :cand_local] for v in found], axis=0)
    out_ref[...] = scores.T

    pltpu.make_async_copy(
        table.at[pl.ds(0, n_dev - 1)], table.at[pl.ds(0, n_dev - 1)], s_send
    ).wait()
    for k in range(1, n_query):
        q_copy(k).wait_send()


def shards(n_index, n_query, queries, passages, lengths, candidates):
    q_local, q_tok, dim = queries.shape
    blk_local, tokens, _ = passages.shape
    per_group = SUB
    groups = blk_local // per_group
    q_rows = q_local * q_tok
    part = 2 * SUB * q_tok
    halves = q_rows // part
    n_dev = n_index * n_query
    flops = 2 * n_query * q_rows * blk_local * tokens * dim
    hbm = pl.BlockSpec(memory_space=pltpu.HBM)
    vmem = pl.BlockSpec(memory_space=pltpu.VMEM)
    return pl.pallas_call(
        functools.partial(maxsim_kernel, n_index, n_query),
        out_shape=pltpu.VMEM(candidates.shape[::-1], jnp.float32),
        in_specs=[hbm, hbm, hbm, hbm],
        out_specs=vmem,
        scratch_shapes=[
            pltpu.SMEM(lengths.shape, jnp.int32),
            pltpu.VMEM(candidates.shape[::-1], jnp.int32),
            pltpu.VMEM((n_query, q_rows, dim), jnp.bfloat16),
            pltpu.VMEM((groups, per_group * tokens, dim), jnp.bfloat16),
            pltpu.VMEM((dim, part), jnp.bfloat16),
            pltpu.VMEM((2, 2 * blk_local, part // 2), jnp.float32),
            pltpu.VMEM((n_query, halves, SUB, LANES), jnp.float32),
            pltpu.VMEM((n_dev, halves, SUB, LANES), jnp.float32),
            pltpu.VMEM((q_local, LANES), jnp.int32),
            pltpu.SemaphoreType.DMA,
            pltpu.SemaphoreType.DMA((groups,)),
            pltpu.SemaphoreType.DMA((n_query,)),
            pltpu.SemaphoreType.DMA((n_query,)),
            pltpu.SemaphoreType.DMA,
            pltpu.SemaphoreType.DMA,
            pltpu.SemaphoreType.DMA,
            pltpu.SemaphoreType.DMA,
        ],
        compiler_params=pltpu.CompilerParams(
            collective_id=0, has_side_effects=True, vmem_limit_bytes=60 * 1024 * 1024
        ),
        cost_estimate=pl.CostEstimate(
            flops=flops, bytes_accessed=passages.size * 2, transcendentals=0
        ),
        name="maxsim",
    )(
        queries.reshape(q_rows, dim),
        passages.reshape(groups, per_group * tokens, dim),
        lengths,
        candidates.T,
    ).T


def solution(mesh):
    in_specs = (
        P("query", None, None),
        P(("index", "query"), None, None),
        P(("index", "query")),
        P("query", "index"),
    )
    body = functools.partial(shards, mesh.shape["index"], mesh.shape["query"])
    return jax.shard_map(
        body, mesh=mesh, in_specs=in_specs, out_specs=P("query", "index"), check_vma=False
    )
```

```python
import functools

import jax
import jax.numpy as jnp
from jax import lax
from jax.experimental import pallas as pl
from jax.experimental.pallas import tpu as pltpu
from jax.sharding import PartitionSpec as P

MESH = pl.DeviceIdType.MESH
LANES = 128
SUB = 8


def maxsim_kernel(
    n_index,
    n_query,
    q_hbm,
    p_hbm,
    len_hbm,
    cand_hbm,
    out_ref,
    len_ref,
    cand_ref,
    q_buf,
    p_buf,
    qt_buf,
    best,
    sent,
    table,
    wide,
    q_sem,
    p_sem,
    q_send,
    q_recv,
    s_send,
    s_recv,
    len_sem,
    cand_sem,
):
    me_i = lax.axis_index("index")
    me_q = lax.axis_index("query")
    n_dev = n_index * n_query
    my_slot = me_i * n_query + me_q
    groups, rows, dim = p_buf.shape
    blk_local = len_ref.shape[0]
    per_group = blk_local // groups
    tokens = rows // per_group
    q_rows = q_buf.shape[1]
    halves = sent.shape[1]
    part = q_rows // halves
    half = part // 2
    q_tok = half // SUB
    cand_local = cand_ref.shape[0]

    q_in = pltpu.make_async_copy(q_hbm, q_buf.at[0], q_sem)
    q_in.start()
    len_in = pltpu.make_async_copy(len_hbm, len_ref, len_sem)
    len_in.start()

    def p_copy(g):
        return pltpu.make_async_copy(p_hbm.at[g], p_buf.at[g], p_sem.at[g])

    for g in range(groups):
        p_copy(g).start()
    cand_in = pltpu.make_async_copy(cand_hbm, cand_ref, cand_sem)
    cand_in.start()

    barrier = pltpu.get_barrier_semaphore()

    def greet(j, carry):
        other = lax.rem(my_slot + j, n_dev)
        pl.semaphore_signal(
            barrier,
            inc=1,
            device_id=(other // n_query, lax.rem(other, n_query)),
            device_id_type=MESH,
        )
        return carry

    lax.fori_loop(1, n_dev, greet, 0)

    token_pos = lax.broadcasted_iota(jnp.int32, (tokens, dim), 0)
    lane_q = lax.broadcasted_iota(jnp.int32, (SUB, half), 1) // q_tok
    row_q = lax.broadcasted_iota(jnp.int32, (SUB, half), 0)
    mean_w = jnp.where(lane_q == row_q, 1.0 / q_tok, 0.0).astype(jnp.bfloat16)

    def fold_rows(tops):
        row = lax.broadcasted_iota(jnp.int32, tops[0].shape, 0)
        step = SUB // 2
        while len(tops) > 1:
            low = (row & step) == 0
            count = len(tops) // 2
            tops = [
                jnp.maximum(
                    jnp.where(low, tops[i], tops[i + count]),
                    pltpu.roll(jnp.where(low, tops[i + count], tops[i]), step, axis=0)
                    if step * 2 == SUB
                    else jnp.where(
                        low,
                        pltpu.roll(tops[i], SUB - step, axis=0),
                        pltpu.roll(tops[i + count], step, axis=0),
                    ),
                )
                for i in range(count)
            ]
            step //= 2
        return tops[0]

    def score_pass(k, m, side, first, between):
        qt_buf[...] = q_buf[k, pl.ds(pl.multiple_of(m * part, part), part), :].T
        for g in range(groups):
            if first:
                p_copy(g).wait()
                blocks = []
                for b in range(per_group):
                    block = p_buf[g, pl.ds(b * tokens, tokens), :].astype(jnp.float32)
                    live = token_pos < len_ref[g * per_group + b]
                    blocks.append(jnp.where(live, block, block[0:1, :]).astype(jnp.bfloat16))
                group_rows = jnp.concatenate(blocks, axis=0)
                p_buf[g] = group_rows
            else:
                group_rows = p_buf[g]
            similar = jnp.dot(group_rows, qt_buf[...], preferred_element_type=jnp.float32)
            pieces = similar.reshape(per_group, tokens // SUB, SUB, part)
            tops = [jnp.max(pieces[b], axis=0) for b in range(per_group)]
            top = fold_rows(tops)
            best[side, pl.ds(g * per_group, per_group), :] = top[:, :half]
            best[side, pl.ds(blk_local + g * per_group, per_group), :] = top[:, half:]
            if g == 0:
                between()

    def mean_scores(k, m, side):
        all_best = best[side]
        high = all_best.astype(jnp.bfloat16)
        low = (all_best - high.astype(jnp.float32)).astype(jnp.bfloat16)
        dims = (((1,), (1,)), ((), ()))
        sent[k, m] = lax.dot_general(
            mean_w, high, dims, preferred_element_type=jnp.float32
        ) + lax.dot_general(mean_w, low, dims, preferred_element_type=jnp.float32)

    def send_one(k, m, j):
        pltpu.make_async_remote_copy(
            src_ref=sent.at[k, m],
            dst_ref=table.at[my_slot, m],
            send_sem=s_send,
            recv_sem=s_recv,
            device_id=(lax.rem(me_i + j, n_index), lax.rem(me_q + k, n_query)),
            device_id_type=MESH,
        ).start()

    def send_rest(k, m):
        for j in range(1, n_index):
            send_one(k, m, j)

    def send_near(k, m):
        @pl.when(k > 0)
        def _():
            send_one(k, m, 0)

        @pl.when(k == 0)
        def _():
            pltpu.make_async_copy(sent.at[k, m], table.at[my_slot, m], s_recv).start()

    def q_copy(k):
        return pltpu.make_async_remote_copy(
            src_ref=q_buf.at[0],
            dst_ref=q_buf.at[k],
            send_sem=q_send.at[k],
            recv_sem=q_recv.at[k],
            device_id=(me_i, lax.rem(me_q + n_query - k, n_query)),
            device_id_type=MESH,
        )

    q_in.wait()
    len_in.wait()
    score_pass(0, 0, 0, True, lambda: None)
    pl.semaphore_wait(barrier, n_dev - 1)
    for k in range(1, n_query):
        q_copy(k).start()

    def later_pass(step, carry):
        k = step // halves
        m = lax.rem(step, halves)
        old = step - 1
        old_k = old // halves
        old_m = lax.rem(old, halves)

        @pl.when((k > 0) & (m == 0))
        def _():
            q_copy(k).wait_recv()

        mean_scores(old_k, old_m, lax.rem(old, 2))
        score_pass(k, m, lax.rem(step, 2), False, lambda: send_rest(old_k, old_m))
        send_near(old_k, old_m)
        return carry

    passes = n_query * halves
    lax.fori_loop(1, passes, later_pass, 0)
    last_k, last_m = n_query - 1, halves - 1
    mean_scores(last_k, last_m, (passes - 1) % 2)
    send_rest(last_k, last_m)
    send_near(last_k, last_m)

    cand_in.wait()
    wide[...] = jnp.zeros_like(wide)
    wide[:, :cand_local] = cand_ref[...].T
    q_groups = cand_ref.shape[1] // SUB
    ids = [wide[pl.ds(g * SUB, SUB), :] for g in range(q_groups)]
    owners = [v // blk_local for v in ids]
    lanes = [
        v - o * blk_local + (g % 2) * blk_local for g, (v, o) in enumerate(zip(ids, owners))
    ]

    pltpu.make_async_copy(table, table, s_recv).wait()

    def pick(o, found):
        here = [table[o, m] for m in range(halves)]
        return tuple(
            jnp.where(
                owners[g] == o,
                jnp.take_along_axis(here[g // 2], lanes[g], axis=1),
                found[g],
            )
            for g in range(q_groups)
        )

    found = lax.fori_loop(
        0, n_dev, pick, tuple(jnp.zeros((SUB, LANES), jnp.float32) for _ in ids), unroll=8
    )
    scores = jnp.concatenate([v[:, :cand_local] for v in found], axis=0)
    out_ref[...] = scores.T

    pltpu.make_async_copy(
        table.at[pl.ds(0, n_dev - 1)], table.at[pl.ds(0, n_dev - 1)], s_send
    ).wait()
    for k in range(1, n_query):
        q_copy(k).wait_send()


def shards(n_index, n_query, queries, passages, lengths, candidates):
    q_local, q_tok, dim = queries.shape
    blk_local, tokens, _ = passages.shape
    per_group = SUB
    groups = blk_local // per_group
    q_rows = q_local * q_tok
    part = 2 * SUB * q_tok
    halves = q_rows // part
    n_dev = n_index * n_query
    flops = 2 * n_query * q_rows * blk_local * tokens * dim
    hbm = pl.BlockSpec(memory_space=pltpu.HBM)
    vmem = pl.BlockSpec(memory_space=pltpu.VMEM)
    return pl.pallas_call(
        functools.partial(maxsim_kernel, n_index, n_query),
        out_shape=pltpu.VMEM(candidates.shape[::-1], jnp.float32),
        in_specs=[hbm, hbm, hbm, hbm],
        out_specs=vmem,
        scratch_shapes=[
            pltpu.SMEM(lengths.shape, jnp.int32),
            pltpu.VMEM(candidates.shape[::-1], jnp.int32),
            pltpu.VMEM((n_query, q_rows, dim), jnp.bfloat16),
            pltpu.VMEM((groups, per_group * tokens, dim), jnp.bfloat16),
            pltpu.VMEM((dim, part), jnp.bfloat16),
            pltpu.VMEM((2, 2 * blk_local, part // 2), jnp.float32),
            pltpu.VMEM((n_query, halves, SUB, LANES), jnp.float32),
            pltpu.VMEM((n_dev, halves, SUB, LANES), jnp.float32),
            pltpu.VMEM((q_local, LANES), jnp.int32),
            pltpu.SemaphoreType.DMA,
            pltpu.SemaphoreType.DMA((groups,)),
            pltpu.SemaphoreType.DMA((n_query,)),
            pltpu.SemaphoreType.DMA((n_query,)),
            pltpu.SemaphoreType.DMA,
            pltpu.SemaphoreType.DMA,
            pltpu.SemaphoreType.DMA,
            pltpu.SemaphoreType.DMA,
        ],
        compiler_params=pltpu.CompilerParams(
            collective_id=0, has_side_effects=True, vmem_limit_bytes=60 * 1024 * 1024
        ),
        cost_estimate=pl.CostEstimate(
            flops=flops, bytes_accessed=passages.size * 2, transcendentals=0
        ),
        name="maxsim",
    )(
        queries.reshape(q_rows, dim),
        passages.reshape(groups, per_group * tokens, dim),
        lengths,
        candidates.T,
    ).T


def solution(mesh):
    in_specs = (
        P("query", None, None),
        P(("index", "query"), None, None),
        P(("index", "query")),
        P("query", "index"),
    )
    body = functools.partial(shards, mesh.shape["index"], mesh.shape["query"])
    return jax.shard_map(
        body, mesh=mesh, in_specs=in_specs, out_specs=P("query", "index"), check_vma=False
    )
```

```python
import functools

import jax
import jax.numpy as jnp
from jax import lax
from jax.experimental import pallas as pl
from jax.experimental.pallas import tpu as pltpu
from jax.sharding import PartitionSpec as P

MESH = pl.DeviceIdType.MESH
LANES = 128
SUB = 8


def maxsim_kernel(
    n_index,
    n_query,
    q_hbm,
    p_hbm,
    len_hbm,
    cand_hbm,
    out_ref,
    len_ref,
    cand_ref,
    q_buf,
    p_buf,
    qt_buf,
    best,
    sent,
    table,
    wide,
    q_sem,
    p_sem,
    q_send,
    q_recv,
    s_send,
    s_recv,
    len_sem,
    cand_sem,
):
    me_i = lax.axis_index("index")
    me_q = lax.axis_index("query")
    n_dev = n_index * n_query
    my_slot = me_i * n_query + me_q
    groups, rows, dim = p_buf.shape
    blk_local = len_ref.shape[0]
    per_group = blk_local // groups
    tokens = rows // per_group
    q_rows = q_buf.shape[1]
    halves = sent.shape[1]
    part = q_rows // halves
    half = part // 2
    q_tok = half // SUB
    cand_local = cand_ref.shape[0]

    q_in = pltpu.make_async_copy(q_hbm, q_buf.at[0], q_sem)
    q_in.start()
    len_in = pltpu.make_async_copy(len_hbm, len_ref, len_sem)
    len_in.start()

    def p_copy(g):
        return pltpu.make_async_copy(p_hbm.at[g], p_buf.at[g], p_sem.at[g])

    for g in range(groups):
        p_copy(g).start()
    cand_in = pltpu.make_async_copy(cand_hbm, cand_ref, cand_sem)
    cand_in.start()

    barrier = pltpu.get_barrier_semaphore()

    def greet(j, carry):
        other = lax.rem(my_slot + j, n_dev)
        pl.semaphore_signal(
            barrier,
            inc=1,
            device_id=(other // n_query, lax.rem(other, n_query)),
            device_id_type=MESH,
        )
        return carry

    lax.fori_loop(1, n_dev, greet, 0)

    token_pos = lax.broadcasted_iota(jnp.int32, (tokens, dim), 0)
    lane_q = lax.broadcasted_iota(jnp.int32, (SUB, half), 1) // q_tok
    row_q = lax.broadcasted_iota(jnp.int32, (SUB, half), 0)
    mean_w = jnp.where(lane_q == row_q, 1.0 / q_tok, 0.0).astype(jnp.bfloat16)

    def fold_rows(tops):
        row = lax.broadcasted_iota(jnp.int32, tops[0].shape, 0)
        step = SUB // 2
        while len(tops) > 1:
            low = (row & step) == 0
            count = len(tops) // 2
            tops = [
                jnp.maximum(
                    jnp.where(low, tops[i], tops[i + count]),
                    pltpu.roll(jnp.where(low, tops[i + count], tops[i]), step, axis=0)
                    if step * 2 == SUB
                    else jnp.where(
                        low,
                        pltpu.roll(tops[i], SUB - step, axis=0),
                        pltpu.roll(tops[i + count], step, axis=0),
                    ),
                )
                for i in range(count)
            ]
            step //= 2
        return tops[0]

    def score_pass(k, m, side, first, between):
        qt_buf[...] = q_buf[k, pl.ds(pl.multiple_of(m * part, part), part), :].T
        for g in range(groups):
            if first:
                p_copy(g).wait()
                blocks = []
                for b in range(per_group):
                    block = p_buf[g, pl.ds(b * tokens, tokens), :].astype(jnp.float32)
                    live = token_pos < len_ref[g * per_group + b]
                    blocks.append(jnp.where(live, block, block[0:1, :]).astype(jnp.bfloat16))
                group_rows = jnp.concatenate(blocks, axis=0)
                p_buf[g] = group_rows
            else:
                group_rows = p_buf[g]
            for h in range(2):
                similar = jnp.dot(
                    group_rows,
                    qt_buf[:, h * half : (h + 1) * half],
                    preferred_element_type=jnp.float32,
                )
                pieces = similar.reshape(per_group, tokens // SUB, SUB, half)
                tops = [jnp.max(pieces[b], axis=0) for b in range(per_group)]
                best[side, pl.ds(h * blk_local + g * per_group, per_group), :] = fold_rows(tops)
            if g == 0:
                between()

    def mean_scores(k, m, side):
        all_best = best[side]
        high = all_best.astype(jnp.bfloat16)
        low = (all_best - high.astype(jnp.float32)).astype(jnp.bfloat16)
        dims = (((1,), (1,)), ((), ()))
        sent[k, m] = lax.dot_general(
            mean_w, high, dims, preferred_element_type=jnp.float32
        ) + lax.dot_general(mean_w, low, dims, preferred_element_type=jnp.float32)

    def send_one(k, m, j):
        pltpu.make_async_remote_copy(
            src_ref=sent.at[k, m],
            dst_ref=table.at[my_slot, m],
            send_sem=s_send,
            recv_sem=s_recv,
            device_id=(lax.rem(me_i + j, n_index), lax.rem(me_q + k, n_query)),
            device_id_type=MESH,
        ).start()

    def send_rest(k, m):
        for j in range(1, n_index):
            send_one(k, m, j)

    def send_near(k, m):
        @pl.when(k > 0)
        def _():
            send_one(k, m, 0)

        @pl.when(k == 0)
        def _():
            pltpu.make_async_copy(sent.at[k, m], table.at[my_slot, m], s_recv).start()

    def q_copy(k):
        return pltpu.make_async_remote_copy(
            src_ref=q_buf.at[0],
            dst_ref=q_buf.at[k],
            send_sem=q_send.at[k],
            recv_sem=q_recv.at[k],
            device_id=(me_i, lax.rem(me_q + n_query - k, n_query)),
            device_id_type=MESH,
        )

    q_in.wait()
    len_in.wait()
    score_pass(0, 0, 0, True, lambda: None)
    pl.semaphore_wait(barrier, n_dev - 1)
    for k in range(1, n_query):
        q_copy(k).start()

    def later_pass(step, carry):
        k = step // halves
        m = lax.rem(step, halves)
        old = step - 1
        old_k = old // halves
        old_m = lax.rem(old, halves)

        @pl.when((k > 0) & (m == 0))
        def _():
            q_copy(k).wait_recv()

        mean_scores(old_k, old_m, lax.rem(old, 2))
        score_pass(k, m, lax.rem(step, 2), False, lambda: send_rest(old_k, old_m))
        send_near(old_k, old_m)
        return carry

    passes = n_query * halves
    lax.fori_loop(1, passes, later_pass, 0)
    last_k, last_m = n_query - 1, halves - 1
    mean_scores(last_k, last_m, (passes - 1) % 2)
    send_rest(last_k, last_m)
    send_near(last_k, last_m)

    cand_in.wait()
    wide[...] = jnp.zeros_like(wide)
    wide[:, :cand_local] = cand_ref[...].T
    q_groups = cand_ref.shape[1] // SUB
    ids = [wide[pl.ds(g * SUB, SUB), :] for g in range(q_groups)]
    owners = [v // blk_local for v in ids]
    lanes = [
        v - o * blk_local + (g % 2) * blk_local for g, (v, o) in enumerate(zip(ids, owners))
    ]

    pltpu.make_async_copy(table, table, s_recv).wait()

    def pick(o, found):
        here = [table[o, m] for m in range(halves)]
        return tuple(
            jnp.where(
                owners[g] == o,
                jnp.take_along_axis(here[g // 2], lanes[g], axis=1),
                found[g],
            )
            for g in range(q_groups)
        )

    found = lax.fori_loop(
        0, n_dev, pick, tuple(jnp.zeros((SUB, LANES), jnp.float32) for _ in ids), unroll=8
    )
    scores = jnp.concatenate([v[:, :cand_local] for v in found], axis=0)
    out_ref[...] = scores.T

    pltpu.make_async_copy(
        table.at[pl.ds(0, n_dev - 1)], table.at[pl.ds(0, n_dev - 1)], s_send
    ).wait()
    for k in range(1, n_query):
        q_copy(k).wait_send()


def shards(n_index, n_query, queries, passages, lengths, candidates):
    q_local, q_tok, dim = queries.shape
    blk_local, tokens, _ = passages.shape
    per_group = SUB
    groups = blk_local // per_group
    q_rows = q_local * q_tok
    part = 2 * SUB * q_tok
    halves = q_rows // part
    n_dev = n_index * n_query
    flops = 2 * n_query * q_rows * blk_local * tokens * dim
    hbm = pl.BlockSpec(memory_space=pltpu.HBM)
    vmem = pl.BlockSpec(memory_space=pltpu.VMEM)
    return pl.pallas_call(
        functools.partial(maxsim_kernel, n_index, n_query),
        out_shape=pltpu.VMEM(candidates.shape[::-1], jnp.float32),
        in_specs=[hbm, hbm, hbm, hbm],
        out_specs=vmem,
        scratch_shapes=[
            pltpu.SMEM(lengths.shape, jnp.int32),
            pltpu.VMEM(candidates.shape[::-1], jnp.int32),
            pltpu.VMEM((n_query, q_rows, dim), jnp.bfloat16),
            pltpu.VMEM((groups, per_group * tokens, dim), jnp.bfloat16),
            pltpu.VMEM((dim, part), jnp.bfloat16),
            pltpu.VMEM((2, 2 * blk_local, part // 2), jnp.float32),
            pltpu.VMEM((n_query, halves, SUB, LANES), jnp.float32),
            pltpu.VMEM((n_dev, halves, SUB, LANES), jnp.float32),
            pltpu.VMEM((q_local, LANES), jnp.int32),
            pltpu.SemaphoreType.DMA,
            pltpu.SemaphoreType.DMA((groups,)),
            pltpu.SemaphoreType.DMA((n_query,)),
            pltpu.SemaphoreType.DMA((n_query,)),
            pltpu.SemaphoreType.DMA,
            pltpu.SemaphoreType.DMA,
            pltpu.SemaphoreType.DMA,
            pltpu.SemaphoreType.DMA,
        ],
        compiler_params=pltpu.CompilerParams(
            collective_id=0, has_side_effects=True, vmem_limit_bytes=60 * 1024 * 1024
        ),
        cost_estimate=pl.CostEstimate(
            flops=flops, bytes_accessed=passages.size * 2, transcendentals=0
        ),
        name="maxsim",
    )(
        queries.reshape(q_rows, dim),
        passages.reshape(groups, per_group * tokens, dim),
        lengths,
        candidates.T,
    ).T


def solution(mesh):
    in_specs = (
        P("query", None, None),
        P(("index", "query"), None, None),
        P(("index", "query")),
        P("query", "index"),
    )
    body = functools.partial(shards, mesh.shape["index"], mesh.shape["query"])
    return jax.shard_map(
        body, mesh=mesh, in_specs=in_specs, out_specs=P("query", "index"), check_vma=False
    )
```
